256 devices in a mesh: dp: 16 (over y, z_lo), tensor: 16 (over z_hi, x, core).
Axes of the slice: x: 4, y: 4, z: 8 (z_hi: 2, z_lo: 4; z = z_hi * 4 + z_lo), core: 2. Of those that a mesh axis runs over, the one named last changes fastest.
Arguments:
- tokens: bfloat16 [512, 8192], P('dp'), may hold values from -6 to 6
- output_gradient: bfloat16 [512, 8192], P('dp'), may hold values from -6 to 6
- gate_up_weight: bfloat16 [8192, 2, 26624], P('dp', None, 'tensor'), may hold values from -0.0625 to 0.0625
- down_weight: bfloat16 [26624, 8192], P('tensor', 'dp'), may hold values from -0.0390625 to 0.0390625
- adapter_input_factor: bfloat16 [512, 16, 8192], P('tensor', None, 'dp'), may hold values from -0.0625 to 0.0625
- adapter_output_factor: bfloat16 [512, 16, 26624], P('dp', None, 'tensor'), may hold values from -1.5 to 1.5
- request_token_rows: int32 [16, 4], replicated, may hold values from 1 to 16, 32 in all within a row
- request_adapter: int32 [16, 4], replicated, may hold values from 0 to 511
- adapter_table_row: int32 [512], replicated, may hold values from 0 to 511, each once
Outputs:
- layer_output: bfloat16 [512, 8192], P('tensor', 'dp')
- input_gradient: bfloat16 [512, 8192], P('tensor', 'dp')
- adapter_input_gradient: bfloat16 [512, 16, 8192], P('tensor', None, 'dp')
- adapter_output_gradient: bfloat16 [512, 16, 26624], P('dp', None, 'tensor')
The draws below stay inside these ranges and needn't reach their ends.
Inputs may be any that keep to these rules, and one draw needn't show every extreme that they name: Each row of request_token_rows sums to 32, and its largest entry is 16. `adapter_table_row`: every table row from 0 to 511 appears once.
All inputs are finite; a program needn't handle non-finite values.
Results may differ from the reference program's by a relative error of at most 0.0059.
Values may be sent and summed in bfloat16 or wider, within the bound.
No kernel may reach another device: no remote copies, remote signals or barrier semaphores. Data moves between devices by JAX's collectives and lax.ppermute only.
A program may use at most 128 MiB of HBM per device.

```python
import math
import jax
import jax.numpy as jnp
import numpy as np
from jax import lax

MODEL_WIDTH = 8192
HIDDEN_UNITS = 26624
ADAPTER_COUNT = 512
ADAPTER_RANK = 16
REQ_DEV = 4
TOK_DEV = 32
LEN_MAX = 16
TOKENS = 512
N_DP = 16


def set_ends(drawn, key, least, top_value):
    longest = drawn.shape.index(max(drawn.shape))
    spots = []
    for shift in (0, 1):
        where = [jax.random.randint(jax.random.fold_in(key, axis), (), 0, length) for axis, length in enumerate(drawn.shape)]
        where[longest] = (where[longest] + shift) % drawn.shape[longest]
        spots.append(tuple(where))
    return drawn.at[spots[0]].set(least).at[spots[1]].set(top_value)


def block_levels(own_key, dims, cuts, smallest, top_value):
    def one(dim, shards_of):
        draws = jax.random.uniform(jax.random.fold_in(jax.random.fold_in(own_key, 6), dim), (shards_of,), jnp.float32, smallest / len(cuts), top_value / len(cuts))
        return jnp.repeat(jnp.exp(draws), dims[dim] // shards_of).reshape((-1,) + (1,) * (len(dims) - dim - 1))

    loudness = one(*cuts[0])
    for cut in cuts[1:]:
        loudness = loudness * one(*cut)
    return loudness


def length_profile(count, total, bound, lean):
    portions = [(1 << 20) // math.isqrt(standing ** lean) + 1 for standing in range(2, count + 1)]
    rest, holding = total - bound - (count - 1), [1] * (count - 1)
    while rest > 0:
        movable = [i for i in range(count - 1) if holding[i] < bound]
        whole, left = sum([portions[i] for i in movable]), rest
        for i in movable:
            more = min(bound - holding[i], max(1, left * portions[i] // whole), rest)
            holding[i] = holding[i] + more
            rest = rest - more
    return np.array([bound] + holding)


def uneven(rng, amount, total, limit, slope):
    if amount == 2:
        one = jax.random.randint(rng, (), max(1, total - limit), min(limit, total - 1) + 1)
        return jnp.stack([one, total - one])
    tallies = jnp.asarray(length_profile(amount, total, limit, slope), jnp.int32)
    couples = (amount - 1) // 2
    giver, taker = tallies[1:1 + 2 * couples:2], tallies[2:2 + 2 * couples:2]
    margin = jnp.minimum(giver - 1, limit - taker)
    passed = jax.random.randint(jax.random.fold_in(rng, 1), (couples,), 0, 1 << 20) % (margin + 1)
    tallies = tallies.at[1:1 + 2 * couples:2].set(giver - passed).at[2:2 + 2 * couples:2].set(taker + passed)
    return tallies[jax.random.permutation(jax.random.fold_in(rng, 2), amount)]


def bell_draw(stream_key, dims, width, reach, cuts=(), held_as=jnp.bfloat16):
    level = block_levels(stream_key, dims, cuts, -0.22, 0.18) if cuts else 1.0
    values = jax.random.normal(stream_key, dims, jnp.float32) * width * level
    return jnp.minimum(jnp.maximum(values, -reach), reach).astype(held_as)


def setup_inputs(seed: int = 0) -> dict:
    arg_keys = jax.random.split(jax.random.key(seed), 10)
    tokens = bell_draw(arg_keys[0], (TOKENS, MODEL_WIDTH), 1.0, 6.0, ((0, 16),))
    output_gradient = bell_draw(arg_keys[1], (TOKENS, MODEL_WIDTH), 1.0, 6.0, ((0, 16),))
    gate_up_weight = bell_draw(arg_keys[2], (MODEL_WIDTH, 2, HIDDEN_UNITS), MODEL_WIDTH ** -0.5, 0.0625, ((0, 16), (2, 16)))
    down_weight = bell_draw(arg_keys[3], (HIDDEN_UNITS, MODEL_WIDTH), HIDDEN_UNITS ** -0.5, 0.0390625, ((0, 16), (1, 16)))
    adapter_input_factor = bell_draw(arg_keys[4], (ADAPTER_COUNT, ADAPTER_RANK, MODEL_WIDTH), MODEL_WIDTH ** -0.5, 0.0625, ((0, 16), (2, 16)))
    adapter_output_factor = bell_draw(arg_keys[5], (ADAPTER_COUNT, ADAPTER_RANK, HIDDEN_UNITS), ADAPTER_RANK ** -0.5, 1.5, ((0, 16), (2, 16)))
    request_token_rows = jax.vmap(lambda own: uneven(own, REQ_DEV, TOK_DEV, LEN_MAX, 2))(jax.random.split(arg_keys[6], N_DP)).reshape((N_DP, REQ_DEV)).astype(jnp.int32)
    request_adapter = set_ends(jax.random.randint(arg_keys[7], (N_DP, REQ_DEV), 0, ADAPTER_COUNT), jax.random.fold_in(arg_keys[7], 1), 0, ADAPTER_COUNT - 1).astype(jnp.int32)
    adapter_table_row = jax.random.permutation(arg_keys[8], ADAPTER_COUNT).astype(jnp.int32)
    return dict(tokens=tokens, output_gradient=output_gradient, gate_up_weight=gate_up_weight, down_weight=down_weight, adapter_input_factor=adapter_input_factor, adapter_output_factor=adapter_output_factor, request_token_rows=request_token_rows, request_adapter=request_adapter, adapter_table_row=adapter_table_row)


adapter_scale = 0.5


def row_slots(request_token_rows, request_adapter, adapter_table_row, group_rows):
    request_count = request_token_rows.shape[1]
    run_ends = jnp.cumsum(request_token_rows, axis=1).astype(jnp.int32)
    position = jnp.arange(group_rows, dtype=jnp.int32)
    request_of = jnp.sum((run_ends[:, None, :] <= position[None, :, None]).astype(jnp.int32), axis=2).astype(jnp.int32)
    request_ids = jnp.arange(request_count, dtype=jnp.int32)
    adapter_of = jnp.sum(jnp.where(request_of[:, :, None] == request_ids[None, None, :], request_adapter[:, None, :], 0), axis=2).astype(jnp.int32)
    adapter_ids = jnp.arange(adapter_table_row.shape[0], dtype=jnp.int32)
    flat_adapter = adapter_of.reshape(-1)
    return jnp.sum(jnp.where(flat_adapter[:, None] == adapter_ids[None, :], adapter_table_row[None, :], 0), axis=1).astype(jnp.int32)


def reference(tokens, output_gradient, gate_up_weight, down_weight, adapter_input_factor, adapter_output_factor, request_token_rows, request_adapter, adapter_table_row):
    groups = request_token_rows.shape[0]
    group_rows = tokens.shape[0] // groups
    slot_of = row_slots(request_token_rows, request_adapter, adapter_table_row, group_rows)
    table_row_blocks = slot_of.reshape(groups, group_rows)
    token_blocks = tokens.reshape(groups, group_rows, tokens.shape[1])

    def codes_of(block):
        token_row_block, table_row_list = block
        return jnp.einsum("ulq,uq->ul", adapter_input_factor[table_row_list].astype(jnp.float32), token_row_block.astype(jnp.float32))

    codes_total_sum = lax.map(codes_of, (token_blocks, table_row_blocks)).reshape(tokens.shape[0], ADAPTER_RANK)
    code_low = codes_total_sum.astype(jnp.bfloat16)
    code_blocks = code_low.reshape(groups, group_rows, ADAPTER_RANK)

    def lift_of(block):
        codes_per_row, table_row_list = block
        return jnp.einsum("uz,uzv->uv", codes_per_row.astype(jnp.float32), adapter_output_factor[table_row_list].astype(jnp.float32))

    raised_codes = lax.map(lift_of, (code_blocks, table_row_blocks)).reshape(tokens.shape[0], HIDDEN_UNITS)
    gate_pre = jnp.dot(tokens, gate_up_weight[:, 0, :], preferred_element_type=jnp.float32)
    up_activation = jnp.dot(tokens, gate_up_weight[:, 1, :], preferred_element_type=jnp.float32) + adapter_scale * raised_codes
    sigmoid_gate = jax.nn.sigmoid(gate_pre)
    hidden = (gate_pre * sigmoid_gate * up_activation).astype(jnp.bfloat16)
    layer_output = jnp.dot(hidden, down_weight, preferred_element_type=jnp.float32).astype(jnp.bfloat16)
    hidden_grad = jnp.dot(output_gradient, down_weight.T, preferred_element_type=jnp.float32)
    gate_grad = (hidden_grad * up_activation * sigmoid_gate * (1.0 + gate_pre * (1.0 - sigmoid_gate))).astype(jnp.bfloat16)
    up_grad = (hidden_grad * gate_pre * sigmoid_gate).astype(jnp.bfloat16)
    up_weight_blocks = up_grad.reshape(groups, group_rows, HIDDEN_UNITS)

    def backward_codes(block):
        up_weight_rows, table_row_list = block
        return jnp.einsum("lb,lhb->lh", up_weight_rows.astype(jnp.float32), adapter_output_factor[table_row_list].astype(jnp.float32))

    codes_gradient = adapter_scale * lax.map(backward_codes, (up_weight_blocks, table_row_blocks)).reshape(tokens.shape[0], ADAPTER_RANK)
    code_grad_low = codes_gradient.astype(jnp.bfloat16)
    gradient_blocks = code_grad_low.reshape(groups, group_rows, ADAPTER_RANK)

    def backward_input(block):
        gradient_rows, table_row_list = block
        return jnp.einsum("hl,hle->he", gradient_rows.astype(jnp.float32), adapter_input_factor[table_row_list].astype(jnp.float32))

    adapter_input_rows = lax.map(backward_input, (gradient_blocks, table_row_blocks)).reshape(tokens.shape[0], MODEL_WIDTH)
    input_gradient = (jnp.dot(gate_grad, gate_up_weight[:, 0, :].T, preferred_element_type=jnp.float32)
               + jnp.dot(up_grad, gate_up_weight[:, 1, :].T, preferred_element_type=jnp.float32)
               + adapter_input_rows).astype(jnp.bfloat16)

    def add_grads(running_totals, block):
        input_total, output_total = running_totals
        token_row_block, codes_per_row, gradient_rows, up_weight_rows, table_row_list = block
        input_total = input_total.at[table_row_list].add(jnp.einsum("rk,rd->rkd", gradient_rows.astype(jnp.float32), token_row_block.astype(jnp.float32)))
        output_total = output_total.at[table_row_list].add(jnp.einsum("rk,rf->rkf", codes_per_row.astype(jnp.float32), up_weight_rows.astype(jnp.float32)))
        return (input_total, output_total), None

    start_totals = (jnp.zeros((ADAPTER_COUNT, ADAPTER_RANK, MODEL_WIDTH), jnp.float32), jnp.zeros((ADAPTER_COUNT, ADAPTER_RANK, HIDDEN_UNITS), jnp.float32))
    running_totals, unused = lax.scan(add_grads, start_totals, (token_blocks, code_blocks, gradient_blocks, up_weight_blocks, table_row_blocks))
    adapter_input_gradient = running_totals[0].astype(jnp.bfloat16)
    adapter_output_gradient = (adapter_scale * running_totals[1]).astype(jnp.bfloat16)
    return (layer_output, input_gradient, adapter_input_gradient, adapter_output_gradient)
```

```python
import jax
import jax.numpy as jnp
from jax import lax
from jax.sharding import Mesh
from jax.sharding import PartitionSpec as P

Y, Z, ZH, X, C = "dp_0", "dp_1", "tensor_0", "tensor_1", "tensor_2"
DP = (Y, Z)
TENSOR = (ZH, X, C)
AXES = (Y, Z, ZH, X, C)

bf16, f32 = jnp.bfloat16, jnp.float32
adapter_scale = 0.5


def shift(value, axis, step):
    n = lax.axis_size(axis)
    return lax.ppermute(value, axis, [(i, (i + step) % n) for i in range(n)])


def dot(a, b, da, db):
    return lax.dot_general(a, b, (((da,), (db,)), ((), ())), preferred_element_type=f32)


def block(value, dim, index):
    return lax.dynamic_index_in_dim(value, index, dim, keepdims=False)


def sum_over(value, axis):
    got = [shift(value, axis, s) for s in range(1, lax.axis_size(axis))]
    for g in got:
        value = value + g
    return value


def sum_all(value):
    for axis in (Y, Z, X, ZH, C):
        value = sum_over(value, axis)
    return value


def scatter_sum(value, axis, dim):
    n, me = lax.axis_size(axis), lax.axis_index(axis)
    got = [shift(block(value, dim, (me + s) % n).astype(bf16), axis, s) for s in range(1, n)]
    total = block(value, dim, me)
    for g in got:
        total = total + g.astype(f32)
    return total


def row_sums(value):
    f = value.shape[1]
    value = scatter_sum(value.reshape(4, -1, f), Y, 0)
    return scatter_sum(value.reshape(4, -1, f), Z, 0)


def put(buffer, piece, index):
    return lax.dynamic_update_slice(buffer, piece[None], (index, 0, 0))


def all_rows(value):
    r, f = value.shape
    n, z = 4, lax.axis_index(Z)
    buf = put(jnp.zeros((n, r, f), value.dtype), value, z)
    for s in range(1, n):
        buf = put(buf, shift(value, Z, s), (z - s) % n)
    value = buf.reshape(n * r, f)
    r, y = n * r, lax.axis_index(Y)
    h = r // 2
    before, after = shift(value, Y, 1), shift(value, Y, -1)
    far_top, far_low = shift(before[:h], Y, 1), shift(after[h:], Y, -1)
    buf = put(jnp.zeros((n, r, f), value.dtype), value, y)
    buf = put(buf, before, (y - 1) % n)
    buf = put(buf, after, (y + 1) % n)
    far = (y + 2) % n
    buf = lax.dynamic_update_slice(buf, far_top[None], (far, 0, 0))
    buf = lax.dynamic_update_slice(buf, far_low[None], (far, h, 0))
    return buf.reshape(n * r, f)


def tensor_sums(value):
    w = value.shape[1]
    value = value.reshape(2, 4, 2, -1, w)
    value = scatter_sum(value, C, 2)
    value = scatter_sum(value, X, 1)
    return scatter_sum(value, ZH, 0)


def row_slot(request_token_rows, request_adapter, adapter_table_row, group_rows):
    ends = jnp.cumsum(request_token_rows, axis=1)
    starts = ends - request_token_rows
    ids = jnp.arange(adapter_table_row.shape[0], dtype=jnp.int32)
    slot = jnp.sum(jnp.where(request_adapter[:, :, None] == ids, adapter_table_row, 0), axis=2)
    p = jnp.arange(group_rows, dtype=jnp.int32)[None, :, None]
    inside = (starts[:, None, :] <= p) & (p < ends[:, None, :])
    return jnp.sum(jnp.where(inside, slot[:, None, :], 0), axis=2).reshape(1, -1)


def on_device(
    tokens,
    output_gradient,
    gate_up_weight,
    down_weight,
    adapter_input_factor,
    adapter_output_factor,
    request_token_rows,
    request_adapter,
    adapter_table_row,
):
    group_rows = tokens.shape[0]
    table_rows, rank, width = adapter_input_factor.shape
    hidden_units = down_weight.shape[0]
    core = lax.axis_index(C)

    mine = jnp.where(core == 0, tokens, output_gradient)
    mine = lax.all_to_all(mine, DP, split_axis=1, concat_axis=0, tiled=True)
    other = shift(mine, C, 1)
    token_cols = jnp.where(core == 0, mine, other)
    grad_cols = jnp.where(core == 0, other, mine)

    slot = row_slot(request_token_rows, request_adapter, adapter_table_row, group_rows)
    table_ids = jnp.arange(table_rows, dtype=jnp.int32)[:, None]
    in_mask = slot == lax.axis_index(TENSOR) * table_rows + table_ids
    out_mask = slot == lax.axis_index(DP) * table_rows + table_ids

    in_factor = adapter_input_factor.reshape(table_rows * rank, width)
    out_factor = adapter_output_factor.reshape(table_rows * rank, hidden_units)
    gate_weight, up_weight = gate_up_weight[:, 0, :], gate_up_weight[:, 1, :]

    def picked(full, mask):
        full = full.reshape(table_rows, rank, -1)
        return jnp.sum(jnp.where(mask[:, None, :], full, 0.0), axis=0)

    def spread(codes, mask):
        out = jnp.where(mask[:, None, :], codes[None], jnp.zeros((), codes.dtype))
        return out.reshape(table_rows * rank, -1)

    codes = sum_all(picked(dot(in_factor, token_cols, 1, 1), in_mask))
    code_low = codes.astype(bf16)
    code_spread = spread(code_low * jnp.asarray(adapter_scale, bf16), out_mask)

    hidden_grad = row_sums(dot(grad_cols, down_weight, 1, 1))
    gate_pre = row_sums(dot(token_cols, gate_weight, 1, 0))
    up_pre = row_sums(dot(token_cols, up_weight, 1, 0) + dot(code_spread, out_factor, 0, 0))

    s = jax.nn.sigmoid(gate_pre)
    silu = gate_pre * s
    up_grad = (hidden_grad * silu).astype(bf16)
    gate_grad = (hidden_grad * up_pre * s * (1.0 + gate_pre * (1.0 - s))).astype(bf16)
    hidden = (silu * up_pre).astype(bf16)

    up_grad = all_rows(up_grad)
    gate_grad = all_rows(gate_grad)
    hidden = all_rows(hidden)

    code_grad = sum_all(picked(dot(out_factor, up_grad, 1, 1), out_mask))
    code_grad_low = (adapter_scale * code_grad).astype(bf16)
    grad_spread = spread(code_grad_low, in_mask)
    adapter_output_gradient = dot(code_spread, up_grad, 1, 0).astype(bf16)
    adapter_input_gradient = dot(grad_spread, token_cols, 1, 0).astype(bf16)

    in_part = (
        dot(gate_grad, gate_weight, 1, 1)
        + dot(up_grad, up_weight, 1, 1)
        + dot(grad_spread, in_factor, 0, 0)
    )
    input_gradient = tensor_sums(in_part).astype(bf16)
    layer_output = tensor_sums(dot(hidden, down_weight, 1, 0)).astype(bf16)
    return (
        layer_output,
        input_gradient,
        adapter_input_gradient.reshape(adapter_input_factor.shape),
        adapter_output_gradient.reshape(adapter_output_factor.shape),
    )


def solution(mesh):
    split = Mesh(mesh.devices.reshape(4, 4, 2, 4, 2), AXES)
    placed = (
        P(DP, None),
        P(DP, None),
        P(DP, None, TENSOR),
        P(TENSOR, DP),
        P(TENSOR, None, DP),
        P(DP, None, TENSOR),
        P(),
        P(),
        P(),
    )
    return jax.shard_map(
        on_device,
        mesh=split,
        in_specs=placed,
        out_specs=(P(TENSOR, DP), P(TENSOR, DP), P(TENSOR, None, DP), P(DP, None, TENSOR)),
        check_vma=False,
    )
```

```python
import jax
import jax.numpy as jnp
from jax import lax
from jax.sharding import Mesh
from jax.sharding import PartitionSpec as P

Y, Z, ZH, X, C = "dp_0", "dp_1", "tensor_0", "tensor_1", "tensor_2"
DP = (Y, Z)
TENSOR = (ZH, X, C)
AXES = (Y, Z, ZH, X, C)

bf16, f32 = jnp.bfloat16, jnp.float32
adapter_scale = 0.5


def shift(value, axis, step):
    n = lax.axis_size(axis)
    return lax.ppermute(value, axis, [(i, (i + step) % n) for i in range(n)])


def dot(a, b, da, db):
    return lax.dot_general(a, b, (((da,), (db,)), ((), ())), preferred_element_type=f32)


def together(*values):
    return lax.optimization_barrier(values)


def block(value, dim, index):
    return lax.dynamic_index_in_dim(value, index, dim, keepdims=False)


def sum_over(value, axis):
    got = [shift(value, axis, s) for s in range(1, lax.axis_size(axis))]
    for g in got:
        value = value + g
    return value


def scatter_sum(value, axis, dim, sent=bf16):
    n, me = lax.axis_size(axis), lax.axis_index(axis)
    got = [shift(block(value, dim, (me + s) % n).astype(sent), axis, s) for s in range(1, n)]
    total = block(value, dim, me)
    for g in got:
        total = total + g.astype(f32)
    return total


def relay_first(value):
    h = value.shape[2] // 2
    far = block(value, 1, (lax.axis_index(Y) + 2) % 4).astype(bf16)
    return shift(far[:, :h], Y, 1), shift(far[:, h:], Y, -1)


def relay_second(value, halves):
    me, h = lax.axis_index(Y), value.shape[2] // 2
    right, left = block(value, 1, (me + 1) % 4), block(value, 1, (me - 1) % 4)
    right = jnp.concatenate([right[:, :h] + halves[0].astype(f32), right[:, h:]], axis=1).astype(bf16)
    left = jnp.concatenate([left[:, :h], left[:, h:] + halves[1].astype(f32)], axis=1).astype(bf16)
    return shift(right, Y, 1), shift(left, Y, -1)


def relay_total(value, arrived):
    return block(value, 1, lax.axis_index(Y)) + arrived[0].astype(f32) + arrived[1].astype(f32)


def quarters(value):
    return value.reshape(value.shape[0], 4, -1, value.shape[2])


def put(buffer, piece, index, row=0):
    return lax.dynamic_update_slice(buffer, piece[:, None], (0, index, row, 0))


def send_z(value):
    return [shift(value, Z, s) for s in range(1, 4)]


def gather_z(value, pieces):
    u, r, f = value.shape
    z = lax.axis_index(Z)
    buf = put(jnp.zeros((u, 4, r, f), value.dtype), value, z)
    for s, piece in enumerate(pieces, 1):
        buf = put(buf, piece, (z - s) % 4)
    return buf.reshape(u, 4 * r, f)


def gather_near(value):
    return shift(value, Y, 1), shift(value, Y, -1)


def gather_far(near):
    h = near[0].shape[1] // 2
    return shift(near[0][:, :h], Y, 1), shift(near[1][:, h:], Y, -1)


def gather_end(value, near, far):
    u, r, f = value.shape
    y = lax.axis_index(Y)
    buf = put(jnp.zeros((u, 4, r, f), value.dtype), value, y)
    buf = put(buf, near[0], (y - 1) % 4)
    buf = put(buf, near[1], (y + 1) % 4)
    buf = put(buf, far[0], (y + 2) % 4)
    buf = put(buf, far[1], (y + 2) % 4, r // 2)
    return buf.reshape(u, 4 * r, f)


def tensor_sums(value):
    u, _, w = value.shape
    value = value.reshape(u, 2, 4, 2, -1, w)
    value = scatter_sum(value, C, 3, f32)
    value = scatter_sum(value, X, 2)
    return scatter_sum(value, ZH, 1)


def row_slot(request_token_rows, request_adapter, adapter_table_row, group_rows):
    ends = jnp.cumsum(request_token_rows, axis=1)
    starts = ends - request_token_rows
    ids = jnp.arange(adapter_table_row.shape[0], dtype=jnp.int32)
    slot = jnp.sum(jnp.where(request_adapter[:, :, None] == ids, adapter_table_row, 0), axis=2)
    p = jnp.arange(group_rows, dtype=jnp.int32)[None, :, None]
    inside = (starts[:, None, :] <= p) & (p < ends[:, None, :])
    return jnp.sum(jnp.where(inside, slot[:, None, :], 0), axis=2).reshape(1, -1)


def on_device(
    tokens,
    output_gradient,
    gate_up_weight,
    down_weight,
    adapter_input_factor,
    adapter_output_factor,
    request_token_rows,
    request_adapter,
    adapter_table_row,
):
    group_rows = tokens.shape[0]
    table_rows, rank, width = adapter_input_factor.shape
    hidden_units = down_weight.shape[0]
    core = lax.axis_index(C)

    mine = jnp.where(core == 0, tokens, output_gradient)
    mine = lax.all_to_all(mine, DP, split_axis=1, concat_axis=0, tiled=True)

    slot = row_slot(request_token_rows, request_adapter, adapter_table_row, group_rows)
    gate_weight, up_weight = gate_up_weight[:, 0, :], gate_up_weight[:, 1, :]
    mine, slot, gate_weight, up_weight = together(mine, slot, gate_weight, up_weight)

    other = shift(mine, C, 1)
    token_cols = jnp.where(core == 0, mine, other)
    grad_cols = jnp.where(core == 0, other, mine)

    table_ids = jnp.arange(table_rows, dtype=jnp.int32)[:, None]
    in_mask = slot == lax.axis_index(TENSOR) * table_rows + table_ids
    out_mask = slot == lax.axis_index(DP) * table_rows + table_ids
    in_factor = adapter_input_factor.reshape(table_rows * rank, width)
    out_factor = adapter_output_factor.reshape(table_rows * rank, hidden_units)

    def picked(full, mask):
        full = full.reshape(table_rows, rank, -1)
        return jnp.sum(jnp.where(mask[:, None, :], full, 0.0), axis=0)

    def spread(codes, mask):
        out = jnp.where(mask[:, None, :], codes[None], jnp.zeros((), codes.dtype))
        return out.reshape(table_rows * rank, -1)

    codes = picked(dot(in_factor, token_cols, 1, 1), in_mask)
    codes, grad_cols = together(codes, grad_cols)
    first = jnp.stack([dot(token_cols, gate_weight, 1, 0), dot(grad_cols, down_weight, 1, 1)])
    first = quarters(first)
    codes, first = together(codes, first)
    halves = relay_first(first)
    codes, halves = together(sum_over(sum_over(codes, Y), Z), halves)
    arrived = relay_second(first, halves)
    codes = sum_over(sum_over(sum_over(codes, X), ZH), C)
    codes, arrived = together(codes, arrived)
    code_low = codes.astype(bf16)
    code_spread = spread(code_low * jnp.asarray(adapter_scale, bf16), out_mask)
    up = dot(token_cols, up_weight, 1, 0) + dot(code_spread, out_factor, 0, 0)
    up = quarters(up[None])
    halves = relay_first(up)
    first = scatter_sum(quarters(relay_total(first, arrived)), Z, 1)
    up = scatter_sum(quarters(relay_total(up, relay_second(up, halves))), Z, 1)

    gate_pre, hidden_grad, up_pre = first[0], first[1], up[0]
    s = jax.nn.sigmoid(gate_pre)
    silu = gate_pre * s
    up_grad = (hidden_grad * silu).astype(bf16)
    gate_grad = (hidden_grad * up_pre * s * (1.0 + gate_pre * (1.0 - s))).astype(bf16)
    hidden = (silu * up_pre).astype(bf16)

    up_grad, both = up_grad[None], jnp.stack([gate_grad, hidden])
    pieces = send_z(up_grad)
    pieces[0], both = together(pieces[0], both)
    up_grad = gather_z(up_grad, pieces)
    both = gather_z(both, send_z(both))
    near = gather_near(up_grad)
    far = gather_far(near)
    first_far, both = together(far[0], both)
    up_grad = gather_end(up_grad, near, (first_far, far[1]))[0]
    near = gather_near(both)
    code_grad = picked(dot(out_factor, up_grad, 1, 1), out_mask)
    code_grad = sum_over(sum_over(code_grad, ZH), Z)
    code_grad, near = together(code_grad, near)
    far = gather_far(near)
    in_part = dot(up_grad, up_weight, 1, 1)
    adapter_output_gradient = dot(code_spread, up_grad, 1, 0).astype(bf16)
    code_grad, far, in_part, adapter_output_gradient = together(
        sum_over(code_grad, X), far, in_part, adapter_output_gradient
    )
    code_grad = sum_over(sum_over(code_grad, Y), C)
    both = gather_end(both, near, far)
    gate_grad, hidden = both[0], both[1]

    code_grad_low = (adapter_scale * code_grad).astype(bf16)
    grad_spread = spread(code_grad_low, in_mask)
    adapter_input_gradient = dot(grad_spread, token_cols, 1, 0).astype(bf16)

    out_part = dot(hidden, down_weight, 1, 0)
    in_part = in_part + dot(gate_grad, gate_weight, 1, 1) + dot(grad_spread, in_factor, 0, 0)
    layer_output, input_gradient = tensor_sums(jnp.stack([out_part, in_part])).astype(bf16)
    return (
        layer_output,
        input_gradient,
        adapter_input_gradient.reshape(adapter_input_factor.shape),
        adapter_output_gradient.reshape(adapter_output_factor.shape),
    )


def solution(mesh):
    split = Mesh(mesh.devices.reshape(4, 4, 2, 4, 2), AXES)
    placed = (
        P(DP, None),
        P(DP, None),
        P(DP, None, TENSOR),
        P(TENSOR, DP),
        P(TENSOR, None, DP),
        P(DP, None, TENSOR),
        P(),
        P(),
        P(),
    )
    return jax.shard_map(
        on_device,
        mesh=split,
        in_specs=placed,
        out_specs=(P(TENSOR, DP), P(TENSOR, DP), P(TENSOR, None, DP), P(DP, None, TENSOR)),
        check_vma=False,
    )
```

```python
import jax
import jax.numpy as jnp
from jax import lax
from jax.sharding import Mesh
from jax.sharding import PartitionSpec as P

Y, Z, ZH, X, C = "dp_0", "dp_1", "tensor_0", "tensor_1", "tensor_2"
DP = (Y, Z)
TENSOR = (ZH, X, C)
AXES = (Y, Z, ZH, X, C)

bf16, f32 = jnp.bfloat16, jnp.float32
adapter_scale = 0.5


def shift(value, axis, step):
    n = lax.axis_size(axis)
    return lax.ppermute(value, axis, [(i, (i + step) % n) for i in range(n)])


def dot(a, b, da, db):
    return lax.dot_general(a, b, (((da,), (db,)), ((), ())), preferred_element_type=f32)


def together(*values):
    return lax.optimization_barrier(values)


def block(value, dim, index):
    return lax.dynamic_index_in_dim(value, index, dim, keepdims=False)


def sum_over(value, axis):
    got = [shift(value, axis, s) for s in range(1, lax.axis_size(axis))]
    for g in got:
        value = value + g
    return value


def scatter_sum(value, axis, dim, sent=bf16):
    n, me = lax.axis_size(axis), lax.axis_index(axis)
    got = [shift(block(value, dim, (me + s) % n).astype(sent), axis, s) for s in range(1, n)]
    total = block(value, dim, me)
    for g in got:
        total = total + g.astype(f32)
    return total


def relay_first(value):
    h = value.shape[2] // 2
    far = block(value, 1, (lax.axis_index(Y) + 2) % 4).astype(bf16)
    return shift(far[:, :h], Y, 1), shift(far[:, h:], Y, -1)


def relay_second(value, halves):
    me, h = lax.axis_index(Y), value.shape[2] // 2
    right, left = block(value, 1, (me + 1) % 4), block(value, 1, (me - 1) % 4)
    right = jnp.concatenate([right[:, :h] + halves[0].astype(f32), right[:, h:]], axis=1).astype(bf16)
    left = jnp.concatenate([left[:, :h], left[:, h:] + halves[1].astype(f32)], axis=1).astype(bf16)
    return shift(right, Y, 1), shift(left, Y, -1)


def relay_total(value, arrived):
    return block(value, 1, lax.axis_index(Y)) + arrived[0].astype(f32) + arrived[1].astype(f32)


def quarters(value):
    return value.reshape(value.shape[0], 4, -1, value.shape[2])


def put(buffer, piece, index, row=0):
    return lax.dynamic_update_slice(buffer, piece[:, None], (0, index, row, 0))


def send_z(value):
    return [shift(value, Z, s) for s in range(1, 4)]


def gather_z(value, pieces):
    u, r, f = value.shape
    z = lax.axis_index(Z)
    buf = put(jnp.zeros((u, 4, r, f), value.dtype), value, z)
    for s, piece in enumerate(pieces, 1):
        buf = put(buf, piece, (z - s) % 4)
    return buf.reshape(u, 4 * r, f)


def gather_y(value, pieces):
    u, r, f = value.shape
    y = lax.axis_index(Y)
    buf = put(jnp.zeros((u, 4, r, f), value.dtype), value, y)
    for s, piece in enumerate(pieces, 1):
        buf = put(buf, piece, (y - s) % 4)
    return buf.reshape(u, 4 * r, f)


def gather_near(value):
    return shift(value, Y, 1), shift(value, Y, -1)


def gather_far(near):
    h = near[0].shape[1] // 2
    return shift(near[0][:, :h], Y, 1), shift(near[1][:, h:], Y, -1)


def gather_end(value, near, far):
    u, r, f = value.shape
    y = lax.axis_index(Y)
    buf = put(jnp.zeros((u, 4, r, f), value.dtype), value, y)
    buf = put(buf, near[0], (y - 1) % 4)
    buf = put(buf, near[1], (y + 1) % 4)
    buf = put(buf, far[0], (y + 2) % 4)
    buf = put(buf, far[1], (y + 2) % 4, r // 2)
    return buf.reshape(u, 4 * r, f)


def tensor_sums(value):
    u, _, w = value.shape
    value = value.reshape(u, 2, 4, 2, -1, w)
    value = scatter_sum(value, C, 3)
    value = scatter_sum(value, X, 2)
    return scatter_sum(value, ZH, 1)


def row_slot(request_token_rows, request_adapter, adapter_table_row, group_rows):
    ends = jnp.cumsum(request_token_rows, axis=1)
    starts = ends - request_token_rows
    ids = jnp.arange(adapter_table_row.shape[0], dtype=jnp.int32)
    slot = jnp.sum(jnp.where(request_adapter[:, :, None] == ids, adapter_table_row, 0), axis=2)
    p = jnp.arange(group_rows, dtype=jnp.int32)[None, :, None]
    inside = (starts[:, None, :] <= p) & (p < ends[:, None, :])
    return jnp.sum(jnp.where(inside, slot[:, None, :], 0), axis=2).reshape(1, -1)


def on_device(
    tokens,
    output_gradient,
    gate_up_weight,
    down_weight,
    adapter_input_factor,
    adapter_output_factor,
    request_token_rows,
    request_adapter,
    adapter_table_row,
):
    group_rows = tokens.shape[0]
    table_rows, rank, width = adapter_input_factor.shape
    hidden_units = down_weight.shape[0]
    core = lax.axis_index(C)

    mine = jnp.where(core == 0, tokens, output_gradient)
    mine = lax.all_to_all(mine, DP, split_axis=1, concat_axis=0, tiled=True)

    slot = row_slot(request_token_rows, request_adapter, adapter_table_row, group_rows)
    gate_weight, up_weight = gate_up_weight[:, 0, :], gate_up_weight[:, 1, :]
    mine, slot, gate_weight, up_weight = together(mine, slot, gate_weight, up_weight)

    other = shift(mine, C, 1)
    token_cols = jnp.where(core == 0, mine, other)
    grad_cols = jnp.where(core == 0, other, mine)

    table_ids = jnp.arange(table_rows, dtype=jnp.int32)[:, None]
    in_mask = slot == lax.axis_index(TENSOR) * table_rows + table_ids
    out_mask = slot == lax.axis_index(DP) * table_rows + table_ids
    in_factor = adapter_input_factor.reshape(table_rows * rank, width)
    out_factor = adapter_output_factor.reshape(table_rows * rank, hidden_units)

    def picked(full, mask):
        full = full.reshape(table_rows, rank, -1)
        return jnp.sum(jnp.where(mask[:, None, :], full, 0.0), axis=0)

    def spread(codes, mask):
        out = jnp.where(mask[:, None, :], codes[None], jnp.zeros((), codes.dtype))
        return out.reshape(table_rows * rank, -1)

    codes = picked(dot(in_factor, token_cols, 1, 1), in_mask)
    codes, grad_cols = together(codes, grad_cols)
    first = jnp.stack([dot(token_cols, gate_weight, 1, 0), dot(grad_cols, down_weight, 1, 1)])
    first = quarters(first)
    codes, first = together(codes, first)
    halves = relay_first(first)
    codes, halves = together(sum_over(sum_over(codes, Y), Z), halves)
    arrived = relay_second(first, halves)
    codes = sum_over(sum_over(sum_over(codes, X), ZH), C)
    codes, arrived = together(codes, arrived)
    code_low = codes.astype(bf16)
    code_spread = spread(code_low * jnp.asarray(adapter_scale, bf16), out_mask)
    up = dot(token_cols, up_weight, 1, 0) + dot(code_spread, out_factor, 0, 0)
    up = quarters(up[None])
    halves = relay_first(up)
    first = scatter_sum(quarters(relay_total(first, arrived)), Z, 1)
    gate_pre, hidden_grad = first[0], first[1]
    s = jax.nn.sigmoid(gate_pre)
    silu = gate_pre * s
    up_grad = (hidden_grad * silu).astype(bf16)[None]
    up = relay_total(up, relay_second(up, halves))
    up_pre = scatter_sum(quarters(up), Z, 1)[0]
    pieces = send_z(up_grad)
    pieces[0], up_pre = together(pieces[0], up_pre)
    up_grad = gather_z(up_grad, pieces)
    gate_grad = (hidden_grad * up_pre * s * (1.0 + gate_pre * (1.0 - s))).astype(bf16)
    hidden = (silu * up_pre).astype(bf16)
    both = jnp.stack([gate_grad, hidden])

    pieces = [shift(up_grad, Y, s) for s in range(1, 4)]
    both = gather_z(both, send_z(both))
    pieces[0], both = together(pieces[0], both)
    up_grad = gather_y(up_grad, pieces)[0]
    near = gather_near(both)
    code_grad = picked(dot(out_factor, up_grad, 1, 1), out_mask)
    code_grad = sum_over(sum_over(code_grad, ZH), Z)
    code_grad, near = together(code_grad, near)
    far = gather_far(near)
    in_part = dot(up_grad, up_weight, 1, 1)
    adapter_output_gradient = dot(code_spread, up_grad, 1, 0).astype(bf16)
    code_grad, far, in_part, adapter_output_gradient = together(
        sum_over(sum_over(code_grad, Y), X), far, in_part, adapter_output_gradient
    )
    code_grad = sum_over(code_grad, C)
    both = gather_end(both, near, far)
    gate_grad, hidden = both[0], both[1]

    code_grad_low = (adapter_scale * code_grad).astype(bf16)
    grad_spread = spread(code_grad_low, in_mask)
    adapter_input_gradient = dot(grad_spread, token_cols, 1, 0).astype(bf16)

    out_part = dot(hidden, down_weight, 1, 0)
    in_part = in_part + dot(gate_grad, gate_weight, 1, 1) + dot(grad_spread, in_factor, 0, 0)
    layer_output, input_gradient = tensor_sums(jnp.stack([out_part, in_part])).astype(bf16)
    return (
        layer_output,
        input_gradient,
        adapter_input_gradient.reshape(adapter_input_factor.shape),
        adapter_output_gradient.reshape(adapter_output_factor.shape),
    )


def solution(mesh):
    split = Mesh(mesh.devices.reshape(4, 4, 2, 4, 2), AXES)
    placed = (
        P(DP, None),
        P(DP, None),
        P(DP, None, TENSOR),
        P(TENSOR, DP),
        P(TENSOR, None, DP),
        P(DP, None, TENSOR),
        P(),
        P(),
        P(),
    )
    return jax.shard_map(
        on_device,
        mesh=split,
        in_specs=placed,
        out_specs=(P(TENSOR, DP), P(TENSOR, DP), P(TENSOR, None, DP), P(DP, None, TENSOR)),
        check_vma=False,
    )
```

```python
import jax
import jax.numpy as jnp
from jax import lax
from jax.sharding import Mesh
from jax.sharding import PartitionSpec as P

Y, Z, ZH, X, C = "dp_0", "dp_1", "tensor_0", "tensor_1", "tensor_2"
DP = (Y, Z)
TENSOR = (ZH, X, C)
AXES = (Y, Z, ZH, X, C)

bf16, f32 = jnp.bfloat16, jnp.float32
adapter_scale = 0.5


def shift(value, axis, step):
    n = lax.axis_size(axis)
    return lax.ppermute(value, axis, [(i, (i + step) % n) for i in range(n)])


def dot(a, b, da, db):
    return lax.dot_general(a, b, (((da,), (db,)), ((), ())), preferred_element_type=f32)


def together(*values):
    return lax.optimization_barrier(values)


def block(value, dim, index):
    return lax.dynamic_index_in_dim(value, index, dim, keepdims=False)


def sum_over(value, axis):
    got = [shift(value, axis, s) for s in range(1, lax.axis_size(axis))]
    for g in got:
        value = value + g
    return value


def scatter_sum(value, axis, dim, sent=bf16):
    n, me = lax.axis_size(axis), lax.axis_index(axis)
    got = [shift(block(value, dim, (me + s) % n).astype(sent), axis, s) for s in range(1, n)]
    total = block(value, dim, me)
    for g in got:
        total = total + g.astype(f32)
    return total


def relay_first(value):
    h = value.shape[2] // 2
    far = block(value, 1, (lax.axis_index(Y) + 2) % 4).astype(bf16)
    return shift(far[:, :h], Y, 1), shift(far[:, h:], Y, -1)


def relay_second(value, halves):
    me, h = lax.axis_index(Y), value.shape[2] // 2
    right, left = block(value, 1, (me + 1) % 4), block(value, 1, (me - 1) % 4)
    right = jnp.concatenate([right[:, :h] + halves[0].astype(f32), right[:, h:]], axis=1).astype(bf16)
    left = jnp.concatenate([left[:, :h], left[:, h:] + halves[1].astype(f32)], axis=1).astype(bf16)
    return shift(right, Y, 1), shift(left, Y, -1)


def relay_total(value, arrived):
    return block(value, 1, lax.axis_index(Y)) + arrived[0].astype(f32) + arrived[1].astype(f32)


def quarters(value):
    return value.reshape(value.shape[0], 4, -1, value.shape[2])


def put(buffer, piece, index, row=0):
    return lax.dynamic_update_slice(buffer, piece[:, None], (0, index, row, 0))


def send_z(value):
    return [shift(value, Z, s) for s in range(1, 4)]


def gather_z(value, pieces):
    u, r, f = value.shape
    z = lax.axis_index(Z)
    buf = put(jnp.zeros((u, 4, r, f), value.dtype), value, z)
    for s, piece in enumerate(pieces, 1):
        buf = put(buf, piece, (z - s) % 4)
    return buf.reshape(u, 4 * r, f)


def gather_y(value, pieces):
    u, r, f = value.shape
    y = lax.axis_index(Y)
    buf = put(jnp.zeros((u, 4, r, f), value.dtype), value, y)
    for s, piece in enumerate(pieces, 1):
        buf = put(buf, piece, (y - s) % 4)
    return buf.reshape(u, 4 * r, f)


def gather_near(value):
    return shift(value, Y, 1), shift(value, Y, -1)


def gather_far(near):
    h = near[0].shape[1] // 2
    return shift(near[0][:, :h], Y, 1), shift(near[1][:, h:], Y, -1)


def gather_some(value, near):
    u, r, f = value.shape
    y = lax.axis_index(Y)
    buf = put(jnp.zeros((u, 4, r, f), value.dtype), value, y)
    buf = put(buf, near[0], (y - 1) % 4)
    buf = put(buf, near[1], (y + 1) % 4)
    return buf.reshape(u, 4 * r, f)


def with_far(total, far_rows):
    far = (lax.axis_index(Y) + 2) % 4
    blocks = total.reshape(4, -1, total.shape[1])
    rows = block(blocks, 0, far) + far_rows
    return lax.dynamic_update_slice(blocks, rows[None], (far, 0, 0)).reshape(total.shape)


def tensor_sums(value):
    u, _, w = value.shape
    value = value.reshape(u, 2, 4, 2, -1, w)
    value = scatter_sum(value, C, 3)
    value = scatter_sum(value, X, 2)
    return scatter_sum(value, ZH, 1)


def row_slot(request_token_rows, request_adapter, adapter_table_row, group_rows):
    ends = jnp.cumsum(request_token_rows, axis=1)
    starts = ends - request_token_rows
    ids = jnp.arange(adapter_table_row.shape[0], dtype=jnp.int32)
    slot = jnp.sum(jnp.where(request_adapter[:, :, None] == ids, adapter_table_row, 0), axis=2)
    p = jnp.arange(group_rows, dtype=jnp.int32)[None, :, None]
    inside = (starts[:, None, :] <= p) & (p < ends[:, None, :])
    return jnp.sum(jnp.where(inside, slot[:, None, :], 0), axis=2).reshape(1, -1)


def on_device(
    tokens,
    output_gradient,
    gate_up_weight,
    down_weight,
    adapter_input_factor,
    adapter_output_factor,
    request_token_rows,
    request_adapter,
    adapter_table_row,
):
    group_rows = tokens.shape[0]
    table_rows, rank, width = adapter_input_factor.shape
    hidden_units = down_weight.shape[0]
    core = lax.axis_index(C)

    mine = jnp.where(core == 0, tokens, output_gradient)
    mine = lax.all_to_all(mine, DP, split_axis=1, concat_axis=0, tiled=True)

    slot = row_slot(request_token_rows, request_adapter, adapter_table_row, group_rows)
    gate_weight, up_weight = gate_up_weight[:, 0, :], gate_up_weight[:, 1, :]
    mine, slot, gate_weight, up_weight = together(mine, slot, gate_weight, up_weight)

    other = shift(mine, C, 1)
    token_cols = jnp.where(core == 0, mine, other)
    grad_cols = jnp.where(core == 0, other, mine)

    table_ids = jnp.arange(table_rows, dtype=jnp.int32)[:, None]
    in_mask = slot == lax.axis_index(TENSOR) * table_rows + table_ids
    out_mask = slot == lax.axis_index(DP) * table_rows + table_ids
    in_factor = adapter_input_factor.reshape(table_rows * rank, width)
    out_factor = adapter_output_factor.reshape(table_rows * rank, hidden_units)

    def picked(full, mask):
        full = full.reshape(table_rows, rank, -1)
        return jnp.sum(jnp.where(mask[:, None, :], full, 0.0), axis=0)

    def spread(codes, mask):
        out = jnp.where(mask[:, None, :], codes[None], jnp.zeros((), codes.dtype))
        return out.reshape(table_rows * rank, -1)

    codes = picked(dot(in_factor, token_cols, 1, 1), in_mask)
    codes, grad_cols = together(codes, grad_cols)
    first = jnp.stack([dot(token_cols, gate_weight, 1, 0), dot(grad_cols, down_weight, 1, 1)])
    first = quarters(first)
    codes, first = together(codes, first)
    halves = relay_first(first)
    codes, halves = together(sum_over(sum_over(codes, Y), Z), halves)
    arrived = relay_second(first, halves)
    codes = sum_over(sum_over(sum_over(codes, X), ZH), C)
    codes, arrived = together(codes, arrived)
    code_low = codes.astype(bf16)
    code_spread = spread(code_low * jnp.asarray(adapter_scale, bf16), out_mask)
    up = dot(token_cols, up_weight, 1, 0) + dot(code_spread, out_factor, 0, 0)
    up = quarters(up[None])
    halves = relay_first(up)
    first = scatter_sum(quarters(relay_total(first, arrived)), Z, 1)
    gate_pre, hidden_grad = first[0], first[1]
    s = jax.nn.sigmoid(gate_pre)
    silu = gate_pre * s
    up_grad = (hidden_grad * silu).astype(bf16)[None]
    up = relay_total(up, relay_second(up, halves))
    up_pre = scatter_sum(quarters(up), Z, 1)[0]
    pieces = send_z(up_grad)
    pieces[0], up_pre = together(pieces[0], up_pre)
    up_grad = gather_z(up_grad, pieces)
    gate_grad = (hidden_grad * up_pre * s * (1.0 + gate_pre * (1.0 - s))).astype(bf16)
    hidden = (silu * up_pre).astype(bf16)
    both = jnp.stack([gate_grad, hidden])

    pieces = [shift(up_grad, Y, s) for s in range(1, 4)]
    both = gather_z(both, send_z(both))
    pieces[0], both = together(pieces[0], both)
    up_grad = gather_y(up_grad, pieces)[0]
    near = gather_near(both)
    code_grad = picked(dot(out_factor, up_grad, 1, 1), out_mask)
    code_grad = sum_over(sum_over(code_grad, ZH), Z)
    in_part = dot(up_grad, up_weight, 1, 1)
    code_grad, near, in_part = together(code_grad, near, in_part)
    far = gather_far(near)
    code_grad, some = together(sum_over(code_grad, Y), gather_some(both, near))
    in_part = in_part + dot(some[0], gate_weight, 1, 1)
    out_part = dot(some[1], down_weight, 1, 0)
    adapter_output_gradient = dot(code_spread, up_grad, 1, 0).astype(bf16)
    code_grad, far, in_part, out_part, adapter_output_gradient = together(
        sum_over(code_grad, X), far, in_part, out_part, adapter_output_gradient
    )
    code_grad = sum_over(code_grad, C)
    far = jnp.concatenate(far, axis=1)

    code_grad_low = (adapter_scale * code_grad).astype(bf16)
    grad_spread = spread(code_grad_low, in_mask)
    adapter_input_gradient = dot(grad_spread, token_cols, 1, 0).astype(bf16)

    out_part = with_far(out_part, dot(far[1], down_weight, 1, 0))
    in_part = with_far(in_part, dot(far[0], gate_weight, 1, 1)) + dot(grad_spread, in_factor, 0, 0)
    layer_output, input_gradient = tensor_sums(jnp.stack([out_part, in_part])).astype(bf16)
    return (
        layer_output,
        input_gradient,
        adapter_input_gradient.reshape(adapter_input_factor.shape),
        adapter_output_gradient.reshape(adapter_output_factor.shape),
    )


def solution(mesh):
    split = Mesh(mesh.devices.reshape(4, 4, 2, 4, 2), AXES)
    placed = (
        P(DP, None),
        P(DP, None),
        P(DP, None, TENSOR),
        P(TENSOR, DP),
        P(TENSOR, None, DP),
        P(DP, None, TENSOR),
        P(),
        P(),
        P(),
    )
    return jax.shard_map(
        on_device,
        mesh=split,
        in_specs=placed,
        out_specs=(P(TENSOR, DP), P(TENSOR, DP), P(TENSOR, None, DP), P(DP, None, TENSOR)),
        check_vma=False,
    )
```
